128 devices in a mesh: row: 8 (over x_hi, z), col: 16 (over y, x_lo, core).
Axes of the slice: x: 4 (x_hi: 2, x_lo: 2; x = x_hi * 2 + x_lo), y: 4, z: 4, core: 2. Of those that a mesh axis runs over, the one named last changes fastest.
Arguments:
- inputs: bfloat16 [2048, 12288], P('col', 'row'), may hold values from -0.125 to 0.125
- weight: bfloat16 [12288, 49152], P('row', 'col'), may hold values from -0.02734375 to 0.02734375
- grad_out: bfloat16 [2048, 49152], P('row', 'col'), may hold values from -8 to 8
Outputs:
- input_grad: bfloat16 [2048, 12288], P('col', 'row')
- weight_grad: bfloat16 [12288, 49152], P('row', 'col')
The draws below stay inside these ranges and needn't reach their ends.
All inputs are finite; a program needn't handle non-finite values.
Results may differ from the reference program's by a relative error of at most 0.001.
Values may be sent and summed in bfloat16 or wider, within the bound.
No kernel may reach another device: no remote copies, remote signals or barrier semaphores. Data moves between devices by JAX's collectives and lax.ppermute only.
A program may use at most 128 MiB of HBM per device.

```python
import jax
import jax.numpy as jnp
from jax import lax

D = 12288
FF = 49152
TOKENS = 2048


def spiked(array, key, source, target, parts, factor):
    def block_of(position):
        return (jnp.arange(array.shape[position]) // (array.shape[position] // parts)).reshape((-1,) + (1,) * (array.ndim - 1 - position))

    first = jax.random.permutation(key, parts)[block_of(target)]
    far = (block_of(target) + parts // 2) % parts
    return jnp.where((block_of(source) == first) | (block_of(source) == far), factor * array, array)


def levels(key, shape, shards, smallest, high):
    gain, own = 1.0, jax.random.fold_in(key, 6)
    for position, shards_of in shards:
        steps = jnp.exp(jax.random.uniform(jax.random.fold_in(own, position), (shards_of,), jnp.float32, smallest / len(shards), high / len(shards)))
        gain = gain * jnp.repeat(steps, shape[position] // shards_of).reshape([-1 if axis == position else 1 for axis in range(len(shape))])
    return gain


def centred(own_key, dims, deviation, most, cuts=(), held_as=jnp.bfloat16):
    level = levels(own_key, dims, cuts, -0.22, 0.18) if cuts else 1.0
    result = jax.random.normal(own_key, dims, jnp.float32) * deviation * level
    return jnp.minimum(jnp.maximum(result, -most), most).astype(held_as)


def bell_draw_with(own_key, shape, scale, limit, pieces, heavy, kind=jnp.bfloat16):
    values = scale * jax.random.normal(own_key, shape, jnp.float32)
    if pieces:
        values = values * levels(own_key, shape, pieces, -0.22, 0.18)
    return jnp.clip(spiked(values, jax.random.fold_in(own_key, 3), *heavy), -limit, limit).astype(kind)


def setup_inputs(seed: int = 0) -> dict:
    key_list = jax.random.split(jax.random.key(seed), 4)
    return {
        "inputs": centred(key_list[0], (TOKENS, D), (TOKENS ** -0.5), 0.125, ((0, 16), (1, 8))),
        "weight": centred(key_list[1], (D, FF), FF ** -0.5, 0.02734375, ((0, 8), (1, 16))),
        "grad_out": bell_draw_with(key_list[2], (TOKENS, FF), 1.0, 8.0, ((0, 8), (1, 16)), (1, 0, 16, 2.0)),
    }


def reference(inputs, weight, grad_out):
    summed = lax.dot_general(grad_out, weight, (((1,), (1,)), ((), ())), preferred_element_type=jnp.float32)
    input_grad = summed.astype(jnp.bfloat16)
    weight_grad = jnp.dot(inputs.T, grad_out, preferred_element_type=jnp.float32).astype(jnp.bfloat16)
    return input_grad, weight_grad
```

```python
import functools

import jax
import jax.numpy as jnp
from jax import lax
from jax.experimental import pallas as pl
from jax.experimental.pallas import tpu as pltpu
from jax.sharding import PartitionSpec as P

BF16 = jnp.bfloat16
F32 = jnp.float32
CHUNKS = (64, 64)
HALF = 128
PLANES, DEPTH = 2, 4
ROWS = PLANES * DEPTH
COLS = 16
MIB = 1 << 20


def row_pairs(move):
    pairs = []
    for plane in range(PLANES):
        for z in range(DEPTH):
            to_plane, to_z = move(plane, z)
            pairs.append((plane * DEPTH + z, to_plane % PLANES * DEPTH + to_z % DEPTH))
    return pairs


UP = row_pairs(lambda p, z: (p, z + 1))
DOWN = row_pairs(lambda p, z: (p, z - 1))
CROSS = row_pairs(lambda p, z: (p + 1, z))
CORE = [(c, c ^ 1) for c in range(COLS)]
BESIDE = [(c, c ^ 2) for c in range(COLS)]
CHIP_GROUPS = [[2 * i + c for i in range(ROWS)] for c in range(2)]
Y_GROUPS = [[i + 4 * y for y in range(4)] for i in range(4)]


def fence(*groups):
    flat, tree = jax.tree.flatten(groups)
    return jax.tree.unflatten(tree, lax.optimization_barrier(flat))


NEAR = ((0, 0), (0, 3), (0, 1), (1, 0))
FAR = ((0, 2), (1, 3), (1, 1), (1, 2))


def pieces_of(sizes, j, offsets):
    size, before = sizes[j], 2 * sizes[j - 1] if j else 0
    places = {
        (0, 0): [(("own", j), half * size) for half in range(2)],
        (1, 0): [(("across", j), half * size) for half in range(2)],
        (0, 3): [(("up", j), before + half * size) for half in range(2)],
        (0, 1): [(("down", j), before + half * size) for half in range(2)],
        (1, 3): [(("up", j + 1), half * size) for half in range(2)],
        (1, 1): [(("down", j + 1), half * size) for half in range(2)],
        (0, 2): [(("far_up", j), 0), (("far_down", j), 0)],
        (1, 2): [(("across_far", j), half * size) for half in range(2)],
    }
    return [places[offset] for offset in offsets]


def send(value, move):
    return lax.ppermute(value, "row", move)


def owner(place, plane, z):
    return (place // DEPTH + plane) % PLANES * DEPTH + (place + z) % DEPTH


def units_kernel(pieces, size, place, *refs):
    blocks, (weight, kept, sent, tokens, held, sems, out_sem) = refs[:-7], refs[-7:]
    core, step = place[1], pl.program_id(0)
    out = pltpu.make_async_copy(held, tokens, out_sem)

    @pl.when(step == 0)
    def _():
        copies = []
        for i, halves in enumerate(pieces):
            for half, (array, first) in enumerate(halves):
                side = (core + half) % 2
                start = (side * len(pieces) + i) * size
                copies.append(
                    pltpu.make_async_copy(
                        blocks[array].at[pl.ds(first, size)],
                        held.at[pl.ds(pl.multiple_of(start, 16), size)],
                        sems.at[len(copies)],
                    )
                )
        for copy in copies:
            copy.start()
        for copy in copies:
            copy.wait()
        out.start()

    total = lax.dot_general(
        held[...], weight[...], (((1,), (1,)), ((), ())), preferred_element_type=F32
    )
    rows = kept.shape[0]
    kept[...] = total[:rows]
    sent[...] = total[rows:]

    @pl.when(step == pl.num_programs(0) - 1)
    def _():
        out.wait()


def contract_units(place, arrays, sizes, j, offsets, weight):
    size, pieces = sizes[j], pieces_of(sizes, j, offsets)
    names = list(dict.fromkeys(name for halves in pieces for name, _ in halves))
    pieces = [[(names.index(name), first) for name, first in halves] for halves in pieces]
    features, units = weight.shape
    rows = len(offsets) * size
    tile = 512
    out = pl.pallas_call(
        functools.partial(units_kernel, pieces, size),
        grid=(features // tile,),
        in_specs=[pl.BlockSpec(memory_space=pltpu.SMEM)]
        + [pl.BlockSpec(memory_space=pl.ANY)] * len(names)
        + [pl.BlockSpec((tile, units), lambda n: (n, 0))],
        out_specs=[pl.BlockSpec((rows, tile), lambda n: (0, n))] * 2
        + [pl.BlockSpec(memory_space=pltpu.HBM)],
        out_shape=[jax.ShapeDtypeStruct((rows, features), F32)] * 2
        + [jax.ShapeDtypeStruct((2 * rows, units), BF16)],
        scratch_shapes=[
            pltpu.VMEM((2 * rows, units), BF16),
            pltpu.SemaphoreType.DMA((2 * len(pieces),)),
            pltpu.SemaphoreType.DMA,
        ],
        compiler_params=pltpu.CompilerParams(vmem_limit_bytes=48 * MIB),
        cost_estimate=pl.CostEstimate(
            flops=4 * rows * units * features,
            bytes_accessed=2 * features * units + 4 * rows * units + 8 * rows * features,
            transcendentals=0,
        ),
        name="units",
    )(place, *[arrays[name] for name in names], weight)
    return [half.reshape(len(offsets), size, features) for half in out[:2]] + [out[2]]


def tokens_kernel(groups, place, *refs):
    blocks, (mine, other, out, held, turned, sems, act_sems) = refs[:-7], refs[-7:]
    row, beside = place[0], place[2]
    tile = out.shape[1]
    columns = pl.ds(pl.multiple_of(pl.program_id(0) * tile, tile), tile)
    counts = [2 * len(offsets) * size for _, size, offsets in groups]
    starts = [sum(counts[:i]) for i in range(len(groups))]

    def copies(i):
        base, size, offsets = groups[i]
        made = [
            pltpu.make_async_copy(blocks[i], held.at[pl.ds(starts[i], counts[i])], sems.at[i])
        ]
        at, n = starts[i], sum(2 * len(g[2]) for g in groups[:i])
        for acts in (mine, other):
            for offset in offsets:
                chip = owner(row, *offset)
                first = chip // 2 * 2 * HALF + (chip + beside) % 2 * HALF + base
                made.append(
                    pltpu.make_async_copy(
                        acts.at[pl.ds(pl.multiple_of(first, 16), size)],
                        turned.at[pl.ds(at, size)],
                        act_sems.at[n],
                    )
                )
                at, n = at + size, n + 1
        return made

    def multiply(first, count):
        rows = pl.ds(first, count)
        return lax.dot_general(
            turned[rows], held[rows, columns], (((0,), (0,)), ((), ())), preferred_element_type=F32
        )

    @pl.when(pl.program_id(0) == 0)
    def _():
        for i in range(len(groups)):
            for copy in copies(i):
                copy.start()
        total = None
        for i in range(len(groups)):
            for copy in copies(i):
                copy.wait()
            part = multiply(starts[i], counts[i])
            total = part if total is None else total + part
        out[...] = total.astype(BF16)

    @pl.when(pl.program_id(0) > 0)
    def _():
        out[...] = multiply(0, held.shape[0]).astype(BF16)


def contract_tokens(place, blocks, groups, mine, other):
    tokens, features = 2 * mine.shape[0], mine.shape[1]
    units = blocks[0].shape[1]
    tile = 512
    return pl.pallas_call(
        functools.partial(tokens_kernel, groups),
        grid=(units // tile,),
        in_specs=[pl.BlockSpec(memory_space=pltpu.SMEM)]
        + [pl.BlockSpec(memory_space=pltpu.HBM)] * (len(blocks) + 2),
        out_specs=pl.BlockSpec((features, tile), lambda n: (0, n)),
        out_shape=jax.ShapeDtypeStruct((features, units), BF16),
        scratch_shapes=[
            pltpu.VMEM((tokens, units), BF16),
            pltpu.VMEM((tokens, features), BF16),
            pltpu.SemaphoreType.DMA((len(groups),)),
            pltpu.SemaphoreType.DMA((sum(2 * len(g[2]) for g in groups),)),
        ],
        compiler_params=pltpu.CompilerParams(vmem_limit_bytes=56 * MIB),
        cost_estimate=pl.CostEstimate(
            flops=2 * tokens * units * features,
            bytes_accessed=2 * (tokens * units + tokens * features + features * units),
            transcendentals=0,
        ),
        name="tokens",
    )(place, *blocks, mine, other)


def chips_kernel(order, near_kept, near_got, far_kept, far_got, out):
    @pl.when(pl.program_id(0) < len(NEAR))
    def _():
        out[...] = near_kept[...] + near_got[...]

    @pl.when(pl.program_id(0) >= len(NEAR))
    def _():
        out[...] = far_kept[...] + far_got[...]


def chip_sums(place, near, far):
    (near_kept, near_sent), (far_kept, far_sent) = near, far
    near_got, far_got = (lax.ppermute(sent, "col", CORE) for sent in (near_sent, far_sent))
    _, size, features = near_kept.shape
    order = jnp.stack([owner(place[0], *offset) for offset in NEAR + FAR])
    block = (1, size, features)
    near = pl.BlockSpec(block, lambda i, order: (jnp.minimum(i, 3), 0, 0))
    far = pl.BlockSpec(block, lambda i, order: (jnp.maximum(i - 4, 0), 0, 0))
    return pl.pallas_call(
        chips_kernel,
        grid_spec=pltpu.PrefetchScalarGridSpec(
            num_scalar_prefetch=1,
            grid=(ROWS,),
            in_specs=[near, near, far, far],
            out_specs=pl.BlockSpec(block, lambda i, order: (order[i], 0, 0)),
        ),
        out_shape=jax.ShapeDtypeStruct((ROWS, size, features), F32),
        compiler_params=pltpu.CompilerParams(vmem_limit_bytes=32 * MIB),
        cost_estimate=pl.CostEstimate(
            flops=ROWS * size * features,
            bytes_accessed=12 * ROWS * size * features,
            transcendentals=0,
        ),
        name="chips",
    )(order, near_kept, near_got, far_kept, far_got)


def gather_along_y(rows):
    copies = jnp.concatenate([rows] * 4)
    return lax.all_to_all(copies, "col", 0, 0, axis_index_groups=Y_GROUPS, tiled=True)


def sum_along_y(chip):
    parts = lax.all_to_all(chip, "col", 0, 0, axis_index_groups=Y_GROUPS, tiled=True)
    return jnp.sum(parts.reshape(4, 2, *chip.shape[1:]), axis=0)


def sum_direct(chip):
    parts = lax.all_to_all(chip, "col", 0, 0, axis_index_groups=CHIP_GROUPS, tiled=True)
    return jnp.sum(parts, axis=0).astype(BF16)


def local(inputs, weight, grad_out):
    row, col = lax.axis_index("row"), lax.axis_index("col")
    place = jnp.stack([row, col % 2, col // 2 % 2]).astype(jnp.int32)
    sizes, count = CHUNKS, len(CHUNKS)
    arrays, base = {}, 0
    for j, size in enumerate(sizes):
        own = [grad_out[half * HALF + base : half * HALF + base + size] for half in range(2)]
        arrays["own", j] = jnp.concatenate(own)
        base += size
    gathered, groups = [], []

    def multiply(j, offsets):
        kept, sent, rows = contract_units(place, arrays, sizes, j, offsets, weight)
        gathered.append(rows)
        groups.append((sum(sizes[:j]), sizes[j], offsets))
        return kept, sent

    near, far = [None] * count, [None] * count
    chips = []
    for k in range(count + 1):
        started, extra = [], ()

        def exchange():
            parts = [arrays["across", k - 1]] if k else []
            if k < count:
                parts.append(arrays["own", k])
            both = jnp.concatenate(parts) if len(parts) > 1 else parts[0]
            arrays["up", k], arrays["down", k] = send(both, UP), send(both, DOWN)
            started.extend([("up", k), ("down", k)])

        if k:
            size = sizes[k - 1]
            first = 2 * sizes[k - 2] if k > 1 else 0
            ready = [
                send(arrays["up", k - 1][first : first + size], UP),
                send(arrays["down", k - 1][first + size : first + 2 * size], DOWN),
            ]
            if k == 1:
                extra = [lax.ppermute(inputs, "col", BESIDE)]
            if k == count:
                exchange()
            if k > 1:
                far[k - 2] = multiply(k - 2, FAR)
                chips.append(chip_sums(place, near[k - 2], far[k - 2]))
            ready, extra, arrays["across", k - 1], near[k - 1], rest = fence(
                ready, extra, arrays["across", k - 1], near[k - 1], [arrays["own", min(k, count - 1)]]
            )
            arrays["own", min(k, count - 1)] = rest[0]
            arrays["far_up", k - 1], arrays["far_down", k - 1] = ready
            arrays["across_far", k - 1] = send(jnp.concatenate(ready), CROSS)
            started.append(("across_far", k - 1))
            near[k - 1] = multiply(k - 1, NEAR)
            if k == 1:
                mine = gather_along_y(jnp.concatenate([inputs, extra[0]]))
        if k < count:
            exchange()
            arrays["across", k] = send(arrays["own", k], CROSS)
            started.append(("across", k))
        held = [arrays[name] for name in started]
        later = [arrays["own", k + 1]] if k + 1 < count else []
        extra = [mine] if k == count else []
        held, later, near, extra = fence(held, later, near, extra)
        arrays.update(zip(started, held))
        if later:
            arrays["own", k + 1] = later[0]
        if extra:
            mine = extra[0]
    far[count - 1] = multiply(count - 1, FAR)
    other = lax.ppermute(mine, "col", CORE)
    chip = chip_sums(place, near[-1], far[-1])
    first = jnp.concatenate([sum_along_y(chip) for chip in chips], axis=1)
    chip, mine, other, first = fence(chip, mine, other, first)
    last = sum_direct(chip)
    beside = place[2]
    own = lax.dynamic_index_in_dim(first, beside, 0, keepdims=False)
    others = lax.dynamic_index_in_dim(first, 1 - beside, 0, keepdims=False)
    sums = [(own + lax.ppermute(others, "col", BESIDE)).astype(BF16), last]
    weight_grad = contract_tokens(place, gathered, groups, mine, other)
    input_grad = jnp.concatenate(sums, axis=0)
    return input_grad, weight_grad


def solution(mesh):
    placed = (P("col", "row"), P("row", "col"), P("row", "col"))
    return jax.shard_map(
        local,
        mesh=mesh,
        in_specs=placed,
        out_specs=(P("col", "row"), P("row", "col")),
        check_vma=False,
    )
```

```python
import functools

import jax
import jax.numpy as jnp
from jax import lax
from jax.experimental import pallas as pl
from jax.experimental.pallas import tpu as pltpu
from jax.sharding import PartitionSpec as P

BF16 = jnp.bfloat16
F32 = jnp.float32
CHUNKS = (64, 64)
HALF = 128
PLANES, DEPTH = 2, 4
ROWS = PLANES * DEPTH
COLS = 16
MIB = 1 << 20


def row_pairs(move):
    pairs = []
    for plane in range(PLANES):
        for z in range(DEPTH):
            to_plane, to_z = move(plane, z)
            pairs.append((plane * DEPTH + z, to_plane % PLANES * DEPTH + to_z % DEPTH))
    return pairs


UP = row_pairs(lambda p, z: (p, z + 1))
DOWN = row_pairs(lambda p, z: (p, z - 1))
CROSS = row_pairs(lambda p, z: (p + 1, z))
CORE = [(c, c ^ 1) for c in range(COLS)]
BESIDE = [(c, c ^ 2) for c in range(COLS)]
CHIP_GROUPS = [[2 * i + c for i in range(ROWS)] for c in range(2)]
Y_GROUPS = [[i + 4 * y for y in range(4)] for i in range(4)]


def fence(*groups):
    flat, tree = jax.tree.flatten(groups)
    return jax.tree.unflatten(tree, lax.optimization_barrier(flat))


NEAR = ((0, 0), (0, 3), (0, 1), (1, 0))
FAR = ((0, 2), (1, 3), (1, 1), (1, 2))


def pieces_of(sizes, j, offsets):
    size, before = sizes[j], 2 * sizes[j - 1] if j else 0
    places = {
        (0, 0): [(("own", j), half * size) for half in range(2)],
        (1, 0): [(("across", j), half * size) for half in range(2)],
        (0, 3): [(("up", j), before + half * size) for half in range(2)],
        (0, 1): [(("down", j), before + half * size) for half in range(2)],
        (1, 3): [(("up", j + 1), half * size) for half in range(2)],
        (1, 1): [(("down", j + 1), half * size) for half in range(2)],
        (0, 2): [(("far_up", j), 0), (("far_down", j), 0)],
        (1, 2): [(("across_far", j), half * size) for half in range(2)],
    }
    return [places[offset] for offset in offsets]


def send(value, move):
    return lax.ppermute(value, "row", move)


def owner(place, plane, z):
    return (place // DEPTH + plane) % PLANES * DEPTH + (place + z) % DEPTH


def units_kernel(parts, place, *refs):
    count = len(parts)
    tokens, (held, sems, out_sems) = refs[-3 - count : -3], refs[-3:]
    sums = refs[-3 - 3 * count : -3 - count]
    blocks, weight = refs[: -4 - 3 * count], refs[-4 - 3 * count]
    core, step = place[1], pl.program_id(0)
    spans, start = [], 0
    for size, pieces in parts:
        spans.append((start, 2 * len(pieces) * size))
        start += spans[-1][1]
    outs = [
        pltpu.make_async_copy(held.at[pl.ds(*span)], rows, out_sems.at[i])
        for i, (span, rows) in enumerate(zip(spans, tokens))
    ]

    @pl.when(step == 0)
    def _():
        copies = []
        for (first_row, _), (size, pieces) in zip(spans, parts):
            for i, halves in enumerate(pieces):
                for half, (array, first) in enumerate(halves):
                    side = (core + half) % 2
                    start = first_row + (side * len(pieces) + i) * size
                    copies.append(
                        pltpu.make_async_copy(
                            blocks[array].at[pl.ds(first, size)],
                            held.at[pl.ds(pl.multiple_of(start, 16), size)],
                            sems.at[len(copies)],
                        )
                    )
        for copy in copies:
            copy.start()
        for copy in copies:
            copy.wait()
        for out in outs:
            out.start()

    total = lax.dot_general(
        held[...], weight[...], (((1,), (1,)), ((), ())), preferred_element_type=F32
    )
    for i, (first, rows) in enumerate(spans):
        sums[2 * i][...] = total[first : first + rows // 2]
        sums[2 * i + 1][...] = total[first + rows // 2 : first + rows]

    @pl.when(step == pl.num_programs(0) - 1)
    def _():
        for out in outs:
            out.wait()


def contract_units(place, arrays, sizes, chosen, weight):
    parts = [(sizes[j], pieces_of(sizes, j, offsets)) for j, offsets in chosen]
    names = list(
        dict.fromkeys(name for _, pieces in parts for halves in pieces for name, _ in halves)
    )
    parts = [
        (size, [[(names.index(name), first) for name, first in halves] for halves in pieces])
        for size, pieces in parts
    ]
    features, units = weight.shape
    counts = [size * len(pieces) for size, pieces in parts]
    rows = 2 * sum(counts)
    tile = 512
    out = pl.pallas_call(
        functools.partial(units_kernel, parts),
        grid=(features // tile,),
        in_specs=[pl.BlockSpec(memory_space=pltpu.SMEM)]
        + [pl.BlockSpec(memory_space=pl.ANY)] * len(names)
        + [pl.BlockSpec((tile, units), lambda n: (n, 0))],
        out_specs=[pl.BlockSpec((n, tile), lambda n: (0, n)) for n in counts for _ in range(2)]
        + [pl.BlockSpec(memory_space=pltpu.HBM)] * len(parts),
        out_shape=[jax.ShapeDtypeStruct((n, features), F32) for n in counts for _ in range(2)]
        + [jax.ShapeDtypeStruct((2 * n, units), BF16) for n in counts],
        scratch_shapes=[
            pltpu.VMEM((rows, units), BF16),
            pltpu.SemaphoreType.DMA((sum(2 * len(pieces) for _, pieces in parts),)),
            pltpu.SemaphoreType.DMA((len(parts),)),
        ],
        compiler_params=pltpu.CompilerParams(vmem_limit_bytes=48 * MIB),
        cost_estimate=pl.CostEstimate(
            flops=2 * rows * units * features,
            bytes_accessed=2 * features * units + 4 * rows * units + 4 * rows * features,
            transcendentals=0,
        ),
        name="units",
    )(place, *[arrays[name] for name in names], weight)
    made = []
    for i, (size, pieces) in enumerate(parts):
        shape = (len(pieces), size, features)
        kept, sent = (half.reshape(shape) for half in out[2 * i : 2 * i + 2])
        made.append((kept, sent, out[2 * len(parts) + i]))
    return made


def tokens_kernel(groups, place, *refs):
    blocks, (mine, other, out, held, turned, sems, act_sems) = refs[:-7], refs[-7:]
    row, beside = place[0], place[2]
    tile = out.shape[1]
    columns = pl.ds(pl.multiple_of(pl.program_id(0) * tile, tile), tile)
    counts = [2 * len(offsets) * size for _, size, offsets in groups]
    starts = [sum(counts[:i]) for i in range(len(groups))]

    def copies(i):
        base, size, offsets = groups[i]
        made = [
            pltpu.make_async_copy(blocks[i], held.at[pl.ds(starts[i], counts[i])], sems.at[i])
        ]
        at, n = starts[i], sum(2 * len(g[2]) for g in groups[:i])
        for acts in (mine, other):
            for offset in offsets:
                chip = owner(row, *offset)
                first = chip // 2 * 2 * HALF + (chip + beside) % 2 * HALF + base
                made.append(
                    pltpu.make_async_copy(
                        acts.at[pl.ds(pl.multiple_of(first, 16), size)],
                        turned.at[pl.ds(at, size)],
                        act_sems.at[n],
                    )
                )
                at, n = at + size, n + 1
        return made

    def multiply(first, count):
        rows = pl.ds(first, count)
        return lax.dot_general(
            turned[rows], held[rows, columns], (((0,), (0,)), ((), ())), preferred_element_type=F32
        )

    @pl.when(pl.program_id(0) == 0)
    def _():
        for i in range(len(groups)):
            for copy in copies(i):
                copy.start()
        total = None
        for i in range(len(groups)):
            for copy in copies(i):
                copy.wait()
            part = multiply(starts[i], counts[i])
            total = part if total is None else total + part
        out[...] = total.astype(BF16)

    @pl.when(pl.program_id(0) > 0)
    def _():
        out[...] = multiply(0, held.shape[0]).astype(BF16)


def contract_tokens(place, blocks, groups, mine, other):
    tokens, features = 2 * mine.shape[0], mine.shape[1]
    units = blocks[0].shape[1]
    tile = 512
    return pl.pallas_call(
        functools.partial(tokens_kernel, groups),
        grid=(units // tile,),
        in_specs=[pl.BlockSpec(memory_space=pltpu.SMEM)]
        + [pl.BlockSpec(memory_space=pltpu.HBM)] * (len(blocks) + 2),
        out_specs=pl.BlockSpec((features, tile), lambda n: (0, n)),
        out_shape=jax.ShapeDtypeStruct((features, units), BF16),
        scratch_shapes=[
            pltpu.VMEM((tokens, units), BF16),
            pltpu.VMEM((tokens, features), BF16),
            pltpu.SemaphoreType.DMA((len(groups),)),
            pltpu.SemaphoreType.DMA((sum(2 * len(g[2]) for g in groups),)),
        ],
        compiler_params=pltpu.CompilerParams(vmem_limit_bytes=56 * MIB),
        cost_estimate=pl.CostEstimate(
            flops=2 * tokens * units * features,
            bytes_accessed=2 * (tokens * units + tokens * features + features * units),
            transcendentals=0,
        ),
        name="tokens",
    )(place, *blocks, mine, other)


def chips_kernel(place, near_kept, near_got, far_kept, far_got, out, held, sems):
    copies = []
    sums = ((near_kept, near_got), (far_kept, far_got))
    for i, offset in enumerate(NEAR + FAR):
        kept, got = sums[i // len(NEAR)]
        held[i] = kept[i % len(NEAR)] + got[i % len(NEAR)]
        copies.append(
            pltpu.make_async_copy(held.at[i], out.at[owner(place[0], *offset)], sems.at[i])
        )
        copies[-1].start()
    for copy in copies:
        copy.wait()


def chip_sums(place, near, far):
    (near_kept, near_sent), (far_kept, far_sent) = near, far
    near_got, far_got = (lax.ppermute(sent, "col", CORE) for sent in (near_sent, far_sent))
    size, features = near_kept.shape[1:]
    return pl.pallas_call(
        chips_kernel,
        in_specs=[pl.BlockSpec(memory_space=pltpu.SMEM)]
        + [pl.BlockSpec(memory_space=pltpu.VMEM)] * 4,
        out_specs=pl.BlockSpec(memory_space=pl.ANY),
        out_shape=jax.ShapeDtypeStruct((ROWS, size, features), F32),
        scratch_shapes=[
            pltpu.VMEM((ROWS, size, features), F32),
            pltpu.SemaphoreType.DMA((ROWS,)),
        ],
        compiler_params=pltpu.CompilerParams(vmem_limit_bytes=24 * MIB),
        cost_estimate=pl.CostEstimate(
            flops=ROWS * size * features,
            bytes_accessed=12 * ROWS * size * features,
            transcendentals=0,
        ),
        name="chips",
    )(place, near_kept, near_got, far_kept, far_got)


def sum_direct(chip):
    parts = lax.all_to_all(chip, "col", 0, 0, axis_index_groups=CHIP_GROUPS, tiled=True)
    return jnp.sum(parts, axis=0).astype(BF16)


def local(inputs, weight, grad_out):
    row, col = lax.axis_index("row"), lax.axis_index("col")
    place = jnp.stack([row, col % 2, col // 2 % 2]).astype(jnp.int32)
    sizes, count = CHUNKS, len(CHUNKS)
    arrays, base = {}, 0
    for j, size in enumerate(sizes):
        own = [grad_out[half * HALF + base : half * HALF + base + size] for half in range(2)]
        arrays["own", j] = jnp.concatenate(own)
        base += size
    gathered, groups = [], []

    def multiply(*chosen):
        made = contract_units(place, arrays, sizes, chosen, weight)
        for (j, offsets), (_, _, rows) in zip(chosen, made):
            gathered.append(rows)
            groups.append((sum(sizes[:j]), sizes[j], offsets))
        return [part[:2] for part in made]

    near, far, sums = [None] * count, [None] * count, []
    beside = lax.ppermute(inputs, "col", BESIDE)
    for k in range(count + 1):
        started = []

        def exchange():
            parts = [arrays["across", k - 1]] if k else []
            if k < count:
                parts.append(arrays["own", k])
            both = jnp.concatenate(parts) if len(parts) > 1 else parts[0]
            arrays["up", k], arrays["down", k] = send(both, UP), send(both, DOWN)
            started.extend([("up", k), ("down", k)])

        if k == 0:
            exchange()
            arrays["across", k] = send(arrays["own", k], CROSS)
            pair = jnp.concatenate([inputs, beside])
            copies = jnp.broadcast_to(pair, (4, *pair.shape))
            arrays["up", k], arrays["down", k], copies, arrays["own", 1] = fence(
                arrays["up", k], arrays["down", k], copies, arrays["own", 1]
            )
            mine = lax.all_to_all(copies, "col", 0, 0, axis_index_groups=Y_GROUPS, tiled=True)
            mine = mine.reshape(-1, mine.shape[-1])
            continue
        size = sizes[k - 1]
        first = 2 * sizes[k - 2] if k > 1 else 0
        ready = [
            send(arrays["up", k - 1][first : first + size], UP),
            send(arrays["down", k - 1][first + size : first + 2 * size], DOWN),
        ]
        if k == count:
            exchange()
        made = []
        if k > 1:
            made = multiply((k - 2, FAR))
        last = min(k, count - 1)
        ready, made, arrays["across", k - 1], arrays["own", last] = fence(
            ready, made, arrays["across", k - 1], arrays["own", last]
        )
        if made:
            far[k - 2] = made[0]
            made = [chip_sums(place, near[k - 2], far[k - 2])]
        arrays["far_up", k - 1], arrays["far_down", k - 1] = ready
        arrays["across_far", k - 1] = send(jnp.concatenate(ready), CROSS)
        if k < count:
            started.append(("across_far", k - 1))
        if k == 1:
            near[0] = multiply((0, NEAR))[0]
        if k < count:
            exchange()
            arrays["across", k] = send(arrays["own", k], CROSS)
            started.append(("across", k))
        if k == count:
            started = []
        held = [arrays[name] for name in started]
        later = [arrays["own", k + 1]] if k + 1 < count else []
        extra = [mine] if k == 1 else []
        held, later, near, extra, made = fence(held, later, near, extra, made)
        if k == count:
            near[k - 1] = multiply((k - 1, NEAR))[0]
        sums += [sum_direct(chip) for chip in made]
        arrays.update(zip(started, held))
        if later:
            arrays["own", k + 1] = later[0]
        if extra:
            mine = extra[0]
            other = lax.ppermute(mine, "col", CORE)
    far[count - 1] = multiply((count - 1, FAR))[0]
    chip = chip_sums(place, near[-1], far[-1])
    chip, mine, other = fence(chip, mine, other)
    sums.append(sum_direct(chip))
    weight_grad = contract_tokens(place, gathered, groups, mine, other)
    input_grad = jnp.concatenate(sums, axis=0)
    return input_grad, weight_grad


def solution(mesh):
    placed = (P("col", "row"), P("row", "col"), P("row", "col"))
    return jax.shard_map(
        local,
        mesh=mesh,
        in_specs=placed,
        out_specs=(P("col", "row"), P("row", "col")),
        check_vma=False,
    )
```

```python
import functools

import jax
import jax.numpy as jnp
from jax import lax
from jax.experimental import pallas as pl
from jax.experimental.pallas import tpu as pltpu
from jax.sharding import PartitionSpec as P

BF16 = jnp.bfloat16
F32 = jnp.float32
CHUNKS = (64, 64)
HALF = 128
PLANES, DEPTH = 2, 4
ROWS = PLANES * DEPTH
COLS = 16
MIB = 1 << 20


def row_pairs(move):
    pairs = []
    for plane in range(PLANES):
        for z in range(DEPTH):
            to_plane, to_z = move(plane, z)
            pairs.append((plane * DEPTH + z, to_plane % PLANES * DEPTH + to_z % DEPTH))
    return pairs


UP = row_pairs(lambda p, z: (p, z + 1))
DOWN = row_pairs(lambda p, z: (p, z - 1))
CROSS = row_pairs(lambda p, z: (p + 1, z))
CORE = [(c, c ^ 1) for c in range(COLS)]
BESIDE = [(c, c ^ 2) for c in range(COLS)]
CHIP_GROUPS = [[2 * i + c for i in range(ROWS)] for c in range(2)]
Y_GROUPS = [[i + 4 * y for y in range(4)] for i in range(4)]


def fence(*groups):
    flat, tree = jax.tree.flatten(groups)
    return jax.tree.unflatten(tree, lax.optimization_barrier(flat))


NEAR = ((0, 0), (0, 3), (0, 1), (1, 0))
FAR = ((0, 2), (1, 3), (1, 1), (1, 2))


def pieces_of(sizes, j, offsets):
    size, before = sizes[j], 2 * sizes[j - 1] if j else 0
    places = {
        (0, 0): [(("own", j), half * size) for half in range(2)],
        (1, 0): [(("across", j), half * size) for half in range(2)],
        (0, 3): [(("up", j), before + half * size) for half in range(2)],
        (0, 1): [(("down", j), before + half * size) for half in range(2)],
        (1, 3): [(("up", j + 1), half * size) for half in range(2)],
        (1, 1): [(("down", j + 1), half * size) for half in range(2)],
        (0, 2): [(("far_up", j), 0), (("far_down", j), 0)],
        (1, 2): [(("across_far", j), half * size) for half in range(2)],
    }
    if j == len(sizes) - 1:
        places[1, 2] = [(("last_up", j), 0), (("last_down", j), 0)]
    return [places[offset] for offset in offsets]


def send(value, move):
    return lax.ppermute(value, "row", move)


def owner(place, plane, z):
    return (place // DEPTH + plane) % PLANES * DEPTH + (place + z) % DEPTH


def units_kernel(parts, place, *refs):
    count = len(parts)
    tokens, (held, sems, out_sems) = refs[-3 - count : -3], refs[-3:]
    sums = refs[-3 - 3 * count : -3 - count]
    blocks, weight = refs[: -4 - 3 * count], refs[-4 - 3 * count]
    core, step = place[1], pl.program_id(0)
    spans, start = [], 0
    for size, pieces in parts:
        spans.append((start, 2 * len(pieces) * size))
        start += spans[-1][1]
    outs = [
        pltpu.make_async_copy(held.at[pl.ds(*span)], rows, out_sems.at[i])
        for i, (span, rows) in enumerate(zip(spans, tokens))
    ]

    @pl.when(step == 0)
    def _():
        copies = []
        for (first_row, _), (size, pieces) in zip(spans, parts):
            for i, halves in enumerate(pieces):
                for half, (array, first) in enumerate(halves):
                    side = (core + half) % 2
                    start = first_row + (side * len(pieces) + i) * size
                    copies.append(
                        pltpu.make_async_copy(
                            blocks[array].at[pl.ds(first, size)],
                            held.at[pl.ds(pl.multiple_of(start, 16), size)],
                            sems.at[len(copies)],
                        )
                    )
        for copy in copies:
            copy.start()
        for copy in copies:
            copy.wait()
        for out in outs:
            out.start()

    total = lax.dot_general(
        held[...], weight[...], (((1,), (1,)), ((), ())), preferred_element_type=F32
    )
    for i, (first, rows) in enumerate(spans):
        sums[2 * i][...] = total[first : first + rows // 2]
        sums[2 * i + 1][...] = total[first + rows // 2 : first + rows]

    @pl.when(step == pl.num_programs(0) - 1)
    def _():
        for out in outs:
            out.wait()


def contract_units(place, arrays, sizes, chosen, weight):
    parts = [(sizes[j], pieces_of(sizes, j, offsets)) for j, offsets in chosen]
    names = list(
        dict.fromkeys(name for _, pieces in parts for halves in pieces for name, _ in halves)
    )
    parts = [
        (size, [[(names.index(name), first) for name, first in halves] for halves in pieces])
        for size, pieces in parts
    ]
    features, units = weight.shape
    counts = [size * len(pieces) for size, pieces in parts]
    rows = 2 * sum(counts)
    tile = 512
    out = pl.pallas_call(
        functools.partial(units_kernel, parts),
        grid=(features // tile,),
        in_specs=[pl.BlockSpec(memory_space=pltpu.SMEM)]
        + [pl.BlockSpec(memory_space=pl.ANY)] * len(names)
        + [pl.BlockSpec((tile, units), lambda n: (n, 0))],
        out_specs=[pl.BlockSpec((n, tile), lambda n: (0, n)) for n in counts for _ in range(2)]
        + [pl.BlockSpec(memory_space=pltpu.HBM)] * len(parts),
        out_shape=[jax.ShapeDtypeStruct((n, features), F32) for n in counts for _ in range(2)]
        + [jax.ShapeDtypeStruct((2 * n, units), BF16) for n in counts],
        scratch_shapes=[
            pltpu.VMEM((rows, units), BF16),
            pltpu.SemaphoreType.DMA((sum(2 * len(pieces) for _, pieces in parts),)),
            pltpu.SemaphoreType.DMA((len(parts),)),
        ],
        compiler_params=pltpu.CompilerParams(vmem_limit_bytes=48 * MIB),
        cost_estimate=pl.CostEstimate(
            flops=2 * rows * units * features,
            bytes_accessed=2 * features * units + 4 * rows * units + 4 * rows * features,
            transcendentals=0,
        ),
        name="units",
    )(place, *[arrays[name] for name in names], weight)
    made = []
    for i, (size, pieces) in enumerate(parts):
        shape = (len(pieces), size, features)
        kept, sent = (half.reshape(shape) for half in out[2 * i : 2 * i + 2])
        made.append((kept, sent, out[2 * len(parts) + i]))
    return made


def tokens_kernel(groups, place, *refs):
    blocks, (mine, other, out, held, turned, sems, act_sems) = refs[:-7], refs[-7:]
    row, beside = place[0], place[2]
    tile = out.shape[1]
    columns = pl.ds(pl.multiple_of(pl.program_id(0) * tile, tile), tile)
    counts = [2 * len(offsets) * size for _, size, offsets in groups]
    starts = [sum(counts[:i]) for i in range(len(groups))]

    def copies(i):
        base, size, offsets = groups[i]
        made = [
            pltpu.make_async_copy(blocks[i], held.at[pl.ds(starts[i], counts[i])], sems.at[i])
        ]
        at, n = starts[i], sum(2 * len(g[2]) for g in groups[:i])
        for acts in (mine, other):
            for offset in offsets:
                chip = owner(row, *offset)
                first = chip // 2 * 2 * HALF + (chip + beside) % 2 * HALF + base
                made.append(
                    pltpu.make_async_copy(
                        acts.at[pl.ds(pl.multiple_of(first, 16), size)],
                        turned.at[pl.ds(at, size)],
                        act_sems.at[n],
                    )
                )
                at, n = at + size, n + 1
        return made

    def multiply(first, count):
        rows = pl.ds(first, count)
        return lax.dot_general(
            turned[rows], held[rows, columns], (((0,), (0,)), ((), ())), preferred_element_type=F32
        )

    @pl.when(pl.program_id(0) == 0)
    def _():
        for i in range(len(groups)):
            for copy in copies(i):
                copy.start()
        total = None
        for i in range(len(groups)):
            for copy in copies(i):
                copy.wait()
            part = multiply(starts[i], counts[i])
            total = part if total is None else total + part
        out[...] = total.astype(BF16)

    @pl.when(pl.program_id(0) > 0)
    def _():
        out[...] = multiply(0, held.shape[0]).astype(BF16)


def contract_tokens(place, blocks, groups, mine, other):
    tokens, features = 2 * mine.shape[0], mine.shape[1]
    units = blocks[0].shape[1]
    tile = 512
    return pl.pallas_call(
        functools.partial(tokens_kernel, groups),
        grid=(units // tile,),
        in_specs=[pl.BlockSpec(memory_space=pltpu.SMEM)]
        + [pl.BlockSpec(memory_space=pltpu.HBM)] * (len(blocks) + 2),
        out_specs=pl.BlockSpec((features, tile), lambda n: (0, n)),
        out_shape=jax.ShapeDtypeStruct((features, units), BF16),
        scratch_shapes=[
            pltpu.VMEM((tokens, units), BF16),
            pltpu.VMEM((tokens, features), BF16),
            pltpu.SemaphoreType.DMA((len(groups),)),
            pltpu.SemaphoreType.DMA((sum(2 * len(g[2]) for g in groups),)),
        ],
        compiler_params=pltpu.CompilerParams(vmem_limit_bytes=56 * MIB),
        cost_estimate=pl.CostEstimate(
            flops=2 * tokens * units * features,
            bytes_accessed=2 * (tokens * units + tokens * features + features * units),
            transcendentals=0,
        ),
        name="tokens",
    )(place, *blocks, mine, other)


def chips_kernel(place, near_kept, near_got, far_kept, far_got, out, held, sems):
    copies = []
    sums = ((near_kept, near_got), (far_kept, far_got))
    for i, offset in enumerate(NEAR + FAR):
        kept, got = sums[i // len(NEAR)]
        held[i] = kept[i % len(NEAR)] + got[i % len(NEAR)]
        copies.append(
            pltpu.make_async_copy(held.at[i], out.at[owner(place[0], *offset)], sems.at[i])
        )
        copies[-1].start()
    for copy in copies:
        copy.wait()


def chip_sums(place, near, far):
    (near_kept, near_sent), (far_kept, far_sent) = near, far
    near_got, far_got = (lax.ppermute(sent, "col", CORE) for sent in (near_sent, far_sent))
    size, features = near_kept.shape[1:]
    return pl.pallas_call(
        chips_kernel,
        in_specs=[pl.BlockSpec(memory_space=pltpu.SMEM)]
        + [pl.BlockSpec(memory_space=pltpu.VMEM)] * 4,
        out_specs=pl.BlockSpec(memory_space=pl.ANY),
        out_shape=jax.ShapeDtypeStruct((ROWS, size, features), F32),
        scratch_shapes=[
            pltpu.VMEM((ROWS, size, features), F32),
            pltpu.SemaphoreType.DMA((ROWS,)),
        ],
        compiler_params=pltpu.CompilerParams(vmem_limit_bytes=24 * MIB),
        cost_estimate=pl.CostEstimate(
            flops=ROWS * size * features,
            bytes_accessed=12 * ROWS * size * features,
            transcendentals=0,
        ),
        name="chips",
    )(place, near_kept, near_got, far_kept, far_got)


def sum_direct(chip):
    parts = lax.all_to_all(chip, "col", 0, 0, axis_index_groups=CHIP_GROUPS, tiled=True)
    return jnp.sum(parts, axis=0).astype(BF16)


def local(inputs, weight, grad_out):
    row, col = lax.axis_index("row"), lax.axis_index("col")
    place = jnp.stack([row, col % 2, col // 2 % 2]).astype(jnp.int32)
    sizes, count = CHUNKS, len(CHUNKS)
    arrays, base = {}, 0
    for j, size in enumerate(sizes):
        own = [grad_out[half * HALF + base : half * HALF + base + size] for half in range(2)]
        arrays["own", j] = jnp.concatenate(own)
        base += size
    gathered, groups = [], []

    def multiply(*chosen):
        made = contract_units(place, arrays, sizes, chosen, weight)
        for (j, offsets), (_, _, rows) in zip(chosen, made):
            gathered.append(rows)
            groups.append((sum(sizes[:j]), sizes[j], offsets))
        return [part[:2] for part in made]

    near, far, sums = [None] * count, [None] * count, []
    beside = lax.ppermute(inputs, "col", BESIDE)
    for k in range(count + 1):
        started = []

        def exchange():
            parts = [arrays["across", k - 1]] if k else []
            if k < count:
                parts.append(arrays["own", k])
            both = jnp.concatenate(parts) if len(parts) > 1 else parts[0]
            arrays["up", k], arrays["down", k] = send(both, UP), send(both, DOWN)
            started.extend([("up", k), ("down", k)])

        if k == 0:
            exchange()
            arrays["across", k] = send(arrays["own", k], CROSS)
            pair = jnp.concatenate([inputs, beside])
            copies = jnp.broadcast_to(pair, (4, *pair.shape))
            arrays["up", k], arrays["down", k], copies, arrays["own", 1] = fence(
                arrays["up", k], arrays["down", k], copies, arrays["own", 1]
            )
            mine = lax.all_to_all(copies, "col", 0, 0, axis_index_groups=Y_GROUPS, tiled=True)
            mine = mine.reshape(-1, mine.shape[-1])
            continue
        size = sizes[k - 1]
        first = 2 * sizes[k - 2] if k > 1 else 0
        ready = [
            send(arrays["up", k - 1][first : first + size], UP),
            send(arrays["down", k - 1][first + size : first + 2 * size], DOWN),
        ]
        if k == count:
            exchange()
        made = []
        if k > 1:
            made = multiply((k - 2, FAR))
        last = min(k, count - 1)
        ready, made, arrays["across", k - 1], arrays["own", last] = fence(
            ready, made, arrays["across", k - 1], arrays["own", last]
        )
        if made:
            far[k - 2] = made[0]
            made = [chip_sums(place, near[k - 2], far[k - 2])]
        arrays["far_up", k - 1], arrays["far_down", k - 1] = ready
        if k < count:
            arrays["across_far", k - 1] = send(jnp.concatenate(ready), CROSS)
            started.append(("across_far", k - 1))
        else:
            arrays["last_up", k - 1] = send(arrays["up", k][:size], UP)
            arrays["last_down", k - 1] = send(arrays["down", k][size:], DOWN)
        if k == 1:
            near[0] = multiply((0, NEAR))[0]
        if k < count:
            exchange()
            arrays["across", k] = send(arrays["own", k], CROSS)
            started.append(("across", k))
        if k == count:
            started = []
        held = [arrays[name] for name in started]
        later = [arrays["own", k + 1]] if k + 1 < count else []
        extra = [mine] if k == 1 else []
        held, later, near, extra, made = fence(held, later, near, extra, made)
        if k == count:
            near[k - 1] = multiply((k - 1, NEAR))[0]
        sums += [sum_direct(chip) for chip in made]
        arrays.update(zip(started, held))
        if later:
            arrays["own", k + 1] = later[0]
        if extra:
            mine = extra[0]
            other = lax.ppermute(mine, "col", CORE)
    far[count - 1] = multiply((count - 1, FAR))[0]
    chip = chip_sums(place, near[-1], far[-1])
    chip, mine, other = fence(chip, mine, other)
    sums.append(sum_direct(chip))
    weight_grad = contract_tokens(place, gathered, groups, mine, other)
    input_grad = jnp.concatenate(sums, axis=0)
    return input_grad, weight_grad


def solution(mesh):
    placed = (P("col", "row"), P("row", "col"), P("row", "col"))
    return jax.shard_map(
        local,
        mesh=mesh,
        in_specs=placed,
        out_specs=(P("col", "row"), P("row", "col")),
        check_vma=False,
    )
```

```python
import functools

import jax
import jax.numpy as jnp
from jax import lax
from jax.experimental import pallas as pl
from jax.experimental.pallas import tpu as pltpu
from jax.sharding import PartitionSpec as P

BF16 = jnp.bfloat16
F32 = jnp.float32
CHUNKS = (64, 64)
HALF = 128
PLANES, DEPTH = 2, 4
ROWS = PLANES * DEPTH
COLS = 16
MIB = 1 << 20


def row_pairs(move):
    pairs = []
    for plane in range(PLANES):
        for z in range(DEPTH):
            to_plane, to_z = move(plane, z)
            pairs.append((plane * DEPTH + z, to_plane % PLANES * DEPTH + to_z % DEPTH))
    return pairs


UP = row_pairs(lambda p, z: (p, z + 1))
DOWN = row_pairs(lambda p, z: (p, z - 1))
CROSS = row_pairs(lambda p, z: (p + 1, z))
CORE = [(c, c ^ 1) for c in range(COLS)]
BESIDE = [(c, c ^ 2) for c in range(COLS)]
CHIP_GROUPS = [[2 * i + c for i in range(ROWS)] for c in range(2)]
Y_GROUPS = [[i + 4 * y for y in range(4)] for i in range(4)]


def fence(*groups):
    flat, tree = jax.tree.flatten(groups)
    return jax.tree.unflatten(tree, lax.optimization_barrier(flat))


NEAR = ((0, 0), (0, 3), (0, 1), (1, 0))
FAR = ((0, 2), (1, 3), (1, 1), (1, 2))


def pieces_of(sizes, j, offsets):
    size, before = sizes[j], 2 * sizes[j - 1] if j else 0
    places = {
        (0, 0): [(("own", j), half * size) for half in range(2)],
        (1, 0): [(("across", j), half * size) for half in range(2)],
        (0, 3): [(("up", j), before + half * size) for half in range(2)],
        (0, 1): [(("down", j), before + half * size) for half in range(2)],
        (1, 3): [(("up", j + 1), half * size) for half in range(2)],
        (1, 1): [(("down", j + 1), half * size) for half in range(2)],
        (0, 2): [(("far_up", j), 0), (("far_down", j), 0)],
        (1, 2): [(("across_far", j), half * size) for half in range(2)],
    }
    if j == len(sizes) - 1:
        places[1, 2] = [(("last_up", j), 0), (("last_down", j), 0)]
    return [places[offset] for offset in offsets]


def send(value, move):
    return lax.ppermute(value, "row", move)


def owner(place, plane, z):
    return (place // DEPTH + plane) % PLANES * DEPTH + (place + z) % DEPTH


def units_kernel(parts, place, *refs):
    count = len(parts)
    tokens, (held, sems, out_sems) = refs[-3 - count : -3], refs[-3:]
    sums = refs[-3 - 3 * count : -3 - count]
    blocks, weight = refs[: -4 - 3 * count], refs[-4 - 3 * count]
    core, step = place[1], pl.program_id(0)
    spans, start = [], 0
    for size, pieces in parts:
        spans.append((start, 2 * len(pieces) * size))
        start += spans[-1][1]
    outs = [
        pltpu.make_async_copy(held.at[pl.ds(*span)], rows, out_sems.at[i])
        for i, (span, rows) in enumerate(zip(spans, tokens))
    ]

    @pl.when(step == 0)
    def _():
        copies = []
        for (first_row, _), (size, pieces) in zip(spans, parts):
            for i, halves in enumerate(pieces):
                for half, (array, first) in enumerate(halves):
                    side = (core + half) % 2
                    start = first_row + (side * len(pieces) + i) * size
                    copies.append(
                        pltpu.make_async_copy(
                            blocks[array].at[pl.ds(first, size)],
                            held.at[pl.ds(pl.multiple_of(start, 16), size)],
                            sems.at[len(copies)],
                        )
                    )
        for copy in copies:
            copy.start()
        for copy in copies:
            copy.wait()
        for out in outs:
            out.start()

    total = lax.dot_general(
        held[...], weight[...], (((1,), (1,)), ((), ())), preferred_element_type=F32
    )
    for i, (first, rows) in enumerate(spans):
        sums[2 * i][...] = total[first : first + rows // 2]
        sums[2 * i + 1][...] = total[first + rows // 2 : first + rows]

    @pl.when(step == pl.num_programs(0) - 1)
    def _():
        for out in outs:
            out.wait()


def contract_units(place, arrays, sizes, chosen, weight):
    parts = [(sizes[j], pieces_of(sizes, j, offsets)) for j, offsets in chosen]
    names = list(
        dict.fromkeys(name for _, pieces in parts for halves in pieces for name, _ in halves)
    )
    parts = [
        (size, [[(names.index(name), first) for name, first in halves] for halves in pieces])
        for size, pieces in parts
    ]
    features, units = weight.shape
    counts = [size * len(pieces) for size, pieces in parts]
    rows = 2 * sum(counts)
    tile = 512
    out = pl.pallas_call(
        functools.partial(units_kernel, parts),
        grid=(features // tile,),
        in_specs=[pl.BlockSpec(memory_space=pltpu.SMEM)]
        + [pl.BlockSpec(memory_space=pl.ANY)] * len(names)
        + [pl.BlockSpec((tile, units), lambda n: (n, 0))],
        out_specs=[pl.BlockSpec((n, tile), lambda n: (0, n)) for n in counts for _ in range(2)]
        + [pl.BlockSpec(memory_space=pltpu.HBM)] * len(parts),
        out_shape=[jax.ShapeDtypeStruct((n, features), F32) for n in counts for _ in range(2)]
        + [jax.ShapeDtypeStruct((2 * n, units), BF16) for n in counts],
        scratch_shapes=[
            pltpu.VMEM((rows, units), BF16),
            pltpu.SemaphoreType.DMA((sum(2 * len(pieces) for _, pieces in parts),)),
            pltpu.SemaphoreType.DMA((len(parts),)),
        ],
        compiler_params=pltpu.CompilerParams(vmem_limit_bytes=48 * MIB),
        cost_estimate=pl.CostEstimate(
            flops=2 * rows * units * features,
            bytes_accessed=2 * features * units + 4 * rows * units + 4 * rows * features,
            transcendentals=0,
        ),
        name="units",
    )(place, *[arrays[name] for name in names], weight)
    made = []
    for i, (size, pieces) in enumerate(parts):
        shape = (len(pieces), size, features)
        kept, sent = (half.reshape(shape) for half in out[2 * i : 2 * i + 2])
        made.append((kept, sent, out[2 * len(parts) + i]))
    return made


def tokens_kernel(groups, place, *refs):
    blocks, (mine, other, out, held, turned, sems, act_sems) = refs[:-7], refs[-7:]
    row, beside = place[0], place[2]
    tile = out.shape[1]
    columns = pl.ds(pl.multiple_of(pl.program_id(0) * tile, tile), tile)
    counts = [2 * len(offsets) * size for _, size, offsets in groups]
    starts = [sum(counts[:i]) for i in range(len(groups))]

    def copies(i):
        base, size, offsets = groups[i]
        made = [
            pltpu.make_async_copy(blocks[i], held.at[pl.ds(starts[i], counts[i])], sems.at[i])
        ]
        at, n = starts[i], sum(2 * len(g[2]) for g in groups[:i])
        for acts in (mine, other):
            for offset in offsets:
                chip = owner(row, *offset)
                first = chip // 2 * 2 * HALF + (chip + beside) % 2 * HALF + base
                made.append(
                    pltpu.make_async_copy(
                        acts.at[pl.ds(pl.multiple_of(first, 16), size)],
                        turned.at[pl.ds(at, size)],
                        act_sems.at[n],
                    )
                )
                at, n = at + size, n + 1
        return made

    def multiply(first, count):
        rows = pl.ds(first, count)
        return lax.dot_general(
            turned[rows], held[rows, columns], (((0,), (0,)), ((), ())), preferred_element_type=F32
        )

    @pl.when(pl.program_id(0) == 0)
    def _():
        for i in range(len(groups)):
            for copy in copies(i):
                copy.start()
        total = None
        for i in range(len(groups)):
            for copy in copies(i):
                copy.wait()
            part = multiply(starts[i], counts[i])
            total = part if total is None else total + part
        out[...] = total.astype(BF16)

    @pl.when(pl.program_id(0) > 0)
    def _():
        out[...] = multiply(0, held.shape[0]).astype(BF16)


def contract_tokens(place, blocks, groups, mine, other):
    tokens, features = 2 * mine.shape[0], mine.shape[1]
    units = blocks[0].shape[1]
    tile = 512
    return pl.pallas_call(
        functools.partial(tokens_kernel, groups),
        grid=(units // tile,),
        in_specs=[pl.BlockSpec(memory_space=pltpu.SMEM)]
        + [pl.BlockSpec(memory_space=pltpu.HBM)] * (len(blocks) + 2),
        out_specs=pl.BlockSpec((features, tile), lambda n: (0, n)),
        out_shape=jax.ShapeDtypeStruct((features, units), BF16),
        scratch_shapes=[
            pltpu.VMEM((tokens, units), BF16),
            pltpu.VMEM((tokens, features), BF16),
            pltpu.SemaphoreType.DMA((len(groups),)),
            pltpu.SemaphoreType.DMA((sum(2 * len(g[2]) for g in groups),)),
        ],
        compiler_params=pltpu.CompilerParams(vmem_limit_bytes=56 * MIB),
        cost_estimate=pl.CostEstimate(
            flops=2 * tokens * units * features,
            bytes_accessed=2 * (tokens * units + tokens * features + features * units),
            transcendentals=0,
        ),
        name="tokens",
    )(place, *blocks, mine, other)


def chips_kernel(place, near_kept, near_got, far_kept, far_got, out, held, sems):
    copies = []
    sums = ((near_kept, near_got), (far_kept, far_got))
    for i, offset in enumerate(NEAR + FAR):
        kept, got = sums[i // len(NEAR)]
        held[i] = kept[i % len(NEAR)] + got[i % len(NEAR)]
        copies.append(
            pltpu.make_async_copy(held.at[i], out.at[owner(place[0], *offset)], sems.at[i])
        )
        copies[-1].start()
    for copy in copies:
        copy.wait()


def chip_sums(place, near, far):
    (near_kept, near_sent), (far_kept, far_sent) = near, far
    near_got, far_got = (lax.ppermute(sent, "col", CORE) for sent in (near_sent, far_sent))
    size, features = near_kept.shape[1:]
    return pl.pallas_call(
        chips_kernel,
        in_specs=[pl.BlockSpec(memory_space=pltpu.SMEM)]
        + [pl.BlockSpec(memory_space=pltpu.VMEM)] * 4,
        out_specs=pl.BlockSpec(memory_space=pl.ANY),
        out_shape=jax.ShapeDtypeStruct((ROWS, size, features), F32),
        scratch_shapes=[
            pltpu.VMEM((ROWS, size, features), F32),
            pltpu.SemaphoreType.DMA((ROWS,)),
        ],
        compiler_params=pltpu.CompilerParams(vmem_limit_bytes=24 * MIB),
        cost_estimate=pl.CostEstimate(
            flops=ROWS * size * features,
            bytes_accessed=12 * ROWS * size * features,
            transcendentals=0,
        ),
        name="chips",
    )(place, near_kept, near_got, far_kept, far_got)


def sum_direct(chip):
    parts = lax.all_to_all(chip, "col", 0, 0, axis_index_groups=CHIP_GROUPS, tiled=True)
    return jnp.sum(parts, axis=0).astype(BF16)


def local(inputs, weight, grad_out):
    row, col = lax.axis_index("row"), lax.axis_index("col")
    place = jnp.stack([row, col % 2, col // 2 % 2]).astype(jnp.int32)
    sizes, count = CHUNKS, len(CHUNKS)
    arrays, base = {}, 0
    for j, size in enumerate(sizes):
        own = [grad_out[half * HALF + base : half * HALF + base + size] for half in range(2)]
        arrays["own", j] = jnp.concatenate(own)
        base += size
    gathered, groups = [], []

    def multiply(*chosen):
        made = contract_units(place, arrays, sizes, chosen, weight)
        for (j, offsets), (_, _, rows) in zip(chosen, made):
            gathered.append(rows)
            groups.append((sum(sizes[:j]), sizes[j], offsets))
        return [part[:2] for part in made]

    near, far, sums = [None] * count, [None] * count, []
    beside = lax.ppermute(inputs, "col", BESIDE)
    for k in range(count + 1):
        started = []

        def exchange():
            parts = [arrays["across", k - 1]] if k else []
            if k < count:
                parts.append(arrays["own", k])
            both = jnp.concatenate(parts) if len(parts) > 1 else parts[0]
            arrays["up", k], arrays["down", k] = send(both, UP), send(both, DOWN)
            started.extend([("up", k), ("down", k)])

        if k == 0:
            exchange()
            arrays["across", k] = send(arrays["own", k], CROSS)
            pair = jnp.concatenate([inputs, beside])
            copies = jnp.broadcast_to(pair, (4, *pair.shape))
            arrays["up", k], arrays["down", k], copies, arrays["own", 1] = fence(
                arrays["up", k], arrays["down", k], copies, arrays["own", 1]
            )
            mine = lax.all_to_all(copies, "col", 0, 0, axis_index_groups=Y_GROUPS, tiled=True)
            mine = mine.reshape(-1, mine.shape[-1])
            continue
        size = sizes[k - 1]
        first = 2 * sizes[k - 2] if k > 1 else 0
        ready = [
            send(arrays["up", k - 1][first : first + size], UP),
            send(arrays["down", k - 1][first + size : first + 2 * size], DOWN),
        ]
        if k == count:
            exchange()
        made = []
        if k > 1:
            made = multiply((k - 2, FAR))
        last = min(k, count - 1)
        if k < count:
            ready, arrays["across", k - 1], arrays["own", last] = fence(
                ready, arrays["across", k - 1], arrays["own", last]
            )
        if made:
            far[k - 2] = made[0]
            made = [chip_sums(place, near[k - 2], far[k - 2])]
        arrays["far_up", k - 1], arrays["far_down", k - 1] = ready
        if k < count:
            arrays["across_far", k - 1] = send(jnp.concatenate(ready), CROSS)
            started.append(("across_far", k - 1))
        else:
            arrays["last_up", k - 1] = send(arrays["up", k][:size], UP)
            arrays["last_down", k - 1] = send(arrays["down", k][size:], DOWN)
        if k == 1:
            near[0] = multiply((0, NEAR))[0]
        if k < count:
            exchange()
            arrays["across", k] = send(arrays["own", k], CROSS)
            started.append(("across", k))
        if k == count:
            started = []
        held = [arrays[name] for name in started]
        later = [arrays["own", k + 1]] if k + 1 < count else []
        extra = [mine] if k == 1 else []
        held, later, near, extra, made = fence(held, later, near, extra, made)
        if k == count:
            near[k - 1] = multiply((k - 1, NEAR))[0]
        sums += [sum_direct(chip) for chip in made]
        arrays.update(zip(started, held))
        if later:
            arrays["own", k + 1] = later[0]
        if extra:
            mine = extra[0]
            other = lax.ppermute(mine, "col", CORE)
    far[count - 1] = multiply((count - 1, FAR))[0]
    chip = chip_sums(place, near[-1], far[-1])
    chip, mine, other = fence(chip, mine, other)
    sums.append(sum_direct(chip))
    weight_grad = contract_tokens(place, gathered, groups, mine, other)
    input_grad = jnp.concatenate(sums, axis=0)
    return input_grad, weight_grad


def solution(mesh):
    placed = (P("col", "row"), P("row", "col"), P("row", "col"))
    return jax.shard_map(
        local,
        mesh=mesh,
        in_specs=placed,
        out_specs=(P("col", "row"), P("row", "col")),
        check_vma=False,
    )
```

```python
import functools

import jax
import jax.numpy as jnp
from jax import lax
from jax.experimental import pallas as pl
from jax.experimental.pallas import tpu as pltpu
from jax.sharding import PartitionSpec as P

BF16 = jnp.bfloat16
F32 = jnp.float32
CHUNKS = (64, 64)
HALF = 128
PLANES, DEPTH = 2, 4
ROWS = PLANES * DEPTH
COLS = 16
MIB = 1 << 20


def row_pairs(move):
    pairs = []
    for plane in range(PLANES):
        for z in range(DEPTH):
            to_plane, to_z = move(plane, z)
            pairs.append((plane * DEPTH + z, to_plane % PLANES * DEPTH + to_z % DEPTH))
    return pairs


UP = row_pairs(lambda p, z: (p, z + 1))
DOWN = row_pairs(lambda p, z: (p, z - 1))
CROSS = row_pairs(lambda p, z: (p + 1, z))
CORE = [(c, c ^ 1) for c in range(COLS)]
BESIDE = [(c, c ^ 2) for c in range(COLS)]
CHIP_GROUPS = [[2 * i + c for i in range(ROWS)] for c in range(2)]
Y_GROUPS = [[i + 4 * y for y in range(4)] for i in range(4)]


def fence(*groups):
    flat, tree = jax.tree.flatten(groups)
    return jax.tree.unflatten(tree, lax.optimization_barrier(flat))


NEAR = ((0, 0), (0, 3), (0, 1), (1, 0))
FAR = ((0, 2), (1, 3), (1, 1), (1, 2))


def pieces_of(sizes, j, offsets):
    size, before = sizes[j], 2 * sizes[j - 1] if j else 0
    places = {
        (0, 0): [(("own", j), half * size) for half in range(2)],
        (1, 0): [(("across", j), half * size) for half in range(2)],
        (0, 3): [(("up", j), before + half * size) for half in range(2)],
        (0, 1): [(("down", j), before + half * size) for half in range(2)],
        (1, 3): [(("up", j + 1), half * size) for half in range(2)],
        (1, 1): [(("down", j + 1), half * size) for half in range(2)],
        (0, 2): [(("far_up", j), 0), (("far_down", j), 0)],
        (1, 2): [(("across_far", j), half * size) for half in range(2)],
    }
    if j == len(sizes) - 1:
        places[1, 2] = [(("last_up", j), 0), (("last_down", j), 0)]
    return [places[offset] for offset in offsets]


def send(value, move):
    return lax.ppermute(value, "row", move)


def owner(place, plane, z):
    return (place // DEPTH + plane) % PLANES * DEPTH + (place + z) % DEPTH


def units_kernel(parts, place, *refs):
    count = len(parts)
    tokens, (held, sems, out_sems) = refs[-3 - count : -3], refs[-3:]
    sums = refs[-3 - 3 * count : -3 - count]
    blocks, weight = refs[: -4 - 3 * count], refs[-4 - 3 * count]
    core, step = place[1], pl.program_id(0)
    spans, start = [], 0
    for size, pieces in parts:
        spans.append((start, 2 * len(pieces) * size))
        start += spans[-1][1]
    outs = [
        pltpu.make_async_copy(held.at[pl.ds(*span)], rows, out_sems.at[i])
        for i, (span, rows) in enumerate(zip(spans, tokens))
    ]

    @pl.when(step == 0)
    def _():
        copies = []
        for (first_row, _), (size, pieces) in zip(spans, parts):
            for i, halves in enumerate(pieces):
                for half, (array, first) in enumerate(halves):
                    side = (core + half) % 2
                    start = first_row + (side * len(pieces) + i) * size
                    copies.append(
                        pltpu.make_async_copy(
                            blocks[array].at[pl.ds(first, size)],
                            held.at[pl.ds(pl.multiple_of(start, 16), size)],
                            sems.at[len(copies)],
                        )
                    )
        for copy in copies:
            copy.start()
        for copy in copies:
            copy.wait()
        for out in outs:
            out.start()

    total = lax.dot_general(
        held[...], weight[...], (((1,), (1,)), ((), ())), preferred_element_type=F32
    )
    for i, (first, rows) in enumerate(spans):
        sums[2 * i][...] = total[first : first + rows // 2]
        sums[2 * i + 1][...] = total[first + rows // 2 : first + rows]

    @pl.when(step == pl.num_programs(0) - 1)
    def _():
        for out in outs:
            out.wait()


def contract_units(place, arrays, sizes, chosen, weight):
    parts = [(sizes[j], pieces_of(sizes, j, offsets)) for j, offsets in chosen]
    names = list(
        dict.fromkeys(name for _, pieces in parts for halves in pieces for name, _ in halves)
    )
    parts = [
        (size, [[(names.index(name), first) for name, first in halves] for halves in pieces])
        for size, pieces in parts
    ]
    features, units = weight.shape
    counts = [size * len(pieces) for size, pieces in parts]
    rows = 2 * sum(counts)
    tile = 512
    out = pl.pallas_call(
        functools.partial(units_kernel, parts),
        grid=(features // tile,),
        in_specs=[pl.BlockSpec(memory_space=pltpu.SMEM)]
        + [pl.BlockSpec(memory_space=pl.ANY)] * len(names)
        + [pl.BlockSpec((tile, units), lambda n: (n, 0))],
        out_specs=[pl.BlockSpec((n, tile), lambda n: (0, n)) for n in counts for _ in range(2)]
        + [pl.BlockSpec(memory_space=pltpu.HBM)] * len(parts),
        out_shape=[jax.ShapeDtypeStruct((n, features), F32) for n in counts for _ in range(2)]
        + [jax.ShapeDtypeStruct((2 * n, units), BF16) for n in counts],
        scratch_shapes=[
            pltpu.VMEM((rows, units), BF16),
            pltpu.SemaphoreType.DMA((sum(2 * len(pieces) for _, pieces in parts),)),
            pltpu.SemaphoreType.DMA((len(parts),)),
        ],
        compiler_params=pltpu.CompilerParams(vmem_limit_bytes=48 * MIB),
        cost_estimate=pl.CostEstimate(
            flops=2 * rows * units * features,
            bytes_accessed=2 * features * units + 4 * rows * units + 4 * rows * features,
            transcendentals=0,
        ),
        name="units",
    )(place, *[arrays[name] for name in names], weight)
    made = []
    for i, (size, pieces) in enumerate(parts):
        shape = (len(pieces), size, features)
        kept, sent = (half.reshape(shape) for half in out[2 * i : 2 * i + 2])
        made.append((kept, sent, out[2 * len(parts) + i]))
    return made


def tokens_kernel(groups, place, *refs):
    blocks, (mine, other, out, held, turned, sems, act_sems) = refs[:-7], refs[-7:]
    row, beside = place[0], place[2]
    tile = out.shape[1]
    columns = pl.ds(pl.multiple_of(pl.program_id(0) * tile, tile), tile)
    counts = [2 * len(offsets) * size for _, size, offsets in groups]
    starts = [sum(counts[:i]) for i in range(len(groups))]

    def copies(i):
        base, size, offsets = groups[i]
        made = [
            pltpu.make_async_copy(blocks[i], held.at[pl.ds(starts[i], counts[i])], sems.at[i])
        ]
        at, n = starts[i], sum(2 * len(g[2]) for g in groups[:i])
        for acts in (mine, other):
            for offset in offsets:
                chip = owner(row, *offset)
                first = chip // 2 * 2 * HALF + (chip + beside) % 2 * HALF + base
                made.append(
                    pltpu.make_async_copy(
                        acts.at[pl.ds(pl.multiple_of(first, 16), size)],
                        turned.at[pl.ds(at, size)],
                        act_sems.at[n],
                    )
                )
                at, n = at + size, n + 1
        return made

    def multiply(first, count):
        rows = pl.ds(first, count)
        return lax.dot_general(
            turned[rows], held[rows, columns], (((0,), (0,)), ((), ())), preferred_element_type=F32
        )

    @pl.when(pl.program_id(0) == 0)
    def _():
        for i in range(len(groups)):
            for copy in copies(i):
                copy.start()
        total = None
        for i in range(len(groups)):
            for copy in copies(i):
                copy.wait()
            part = multiply(starts[i], counts[i])
            total = part if total is None else total + part
        out[...] = total.astype(BF16)

    @pl.when(pl.program_id(0) > 0)
    def _():
        out[...] = multiply(0, held.shape[0]).astype(BF16)


def contract_tokens(place, blocks, groups, mine, other):
    tokens, features = 2 * mine.shape[0], mine.shape[1]
    units = blocks[0].shape[1]
    tile = 512
    return pl.pallas_call(
        functools.partial(tokens_kernel, groups),
        grid=(units // tile,),
        in_specs=[pl.BlockSpec(memory_space=pltpu.SMEM)]
        + [pl.BlockSpec(memory_space=pltpu.HBM)] * (len(blocks) + 2),
        out_specs=pl.BlockSpec((features, tile), lambda n: (0, n)),
        out_shape=jax.ShapeDtypeStruct((features, units), BF16),
        scratch_shapes=[
            pltpu.VMEM((tokens, units), BF16),
            pltpu.VMEM((tokens, features), BF16),
            pltpu.SemaphoreType.DMA((len(groups),)),
            pltpu.SemaphoreType.DMA((sum(2 * len(g[2]) for g in groups),)),
        ],
        compiler_params=pltpu.CompilerParams(vmem_limit_bytes=56 * MIB),
        cost_estimate=pl.CostEstimate(
            flops=2 * tokens * units * features,
            bytes_accessed=2 * (tokens * units + tokens * features + features * units),
            transcendentals=0,
        ),
        name="tokens",
    )(place, *blocks, mine, other)


def chips_kernel(place, near_kept, near_got, far_kept, far_got, out, held, sems):
    copies = []
    sums = ((near_kept, near_got), (far_kept, far_got))
    for i, offset in enumerate(NEAR + FAR):
        kept, got = sums[i // len(NEAR)]
        held[i] = kept[i % len(NEAR)] + got[i % len(NEAR)]
        copies.append(
            pltpu.make_async_copy(held.at[i], out.at[owner(place[0], *offset)], sems.at[i])
        )
        copies[-1].start()
    for copy in copies:
        copy.wait()


def chip_sums(place, near, far):
    (near_kept, near_sent), (far_kept, far_sent) = near, far
    near_got, far_got = (lax.ppermute(sent, "col", CORE) for sent in (near_sent, far_sent))
    size, features = near_kept.shape[1:]
    return pl.pallas_call(
        chips_kernel,
        in_specs=[pl.BlockSpec(memory_space=pltpu.SMEM)]
        + [pl.BlockSpec(memory_space=pltpu.VMEM)] * 4,
        out_specs=pl.BlockSpec(memory_space=pl.ANY),
        out_shape=jax.ShapeDtypeStruct((ROWS, size, features), F32),
        scratch_shapes=[
            pltpu.VMEM((ROWS, size, features), F32),
            pltpu.SemaphoreType.DMA((ROWS,)),
        ],
        compiler_params=pltpu.CompilerParams(vmem_limit_bytes=24 * MIB),
        cost_estimate=pl.CostEstimate(
            flops=ROWS * size * features,
            bytes_accessed=12 * ROWS * size * features,
            transcendentals=0,
        ),
        name="chips",
    )(place, near_kept, near_got, far_kept, far_got)


def sum_direct(chip):
    parts = lax.all_to_all(chip, "col", 0, 0, axis_index_groups=CHIP_GROUPS, tiled=True)
    return jnp.sum(parts, axis=0).astype(BF16)


def local(inputs, weight, grad_out):
    row, col = lax.axis_index("row"), lax.axis_index("col")
    place = jnp.stack([row, col % 2, col // 2 % 2]).astype(jnp.int32)
    sizes, count = CHUNKS, len(CHUNKS)
    arrays, base = {}, 0
    for j, size in enumerate(sizes):
        own = [grad_out[half * HALF + base : half * HALF + base + size] for half in range(2)]
        arrays["own", j] = jnp.concatenate(own)
        base += size
    gathered, groups = [], []

    def multiply(*chosen):
        made = contract_units(place, arrays, sizes, chosen, weight)
        for (j, offsets), (_, _, rows) in zip(chosen, made):
            gathered.append(rows)
            groups.append((sum(sizes[:j]), sizes[j], offsets))
        return [part[:2] for part in made]

    near, far, sums = [None] * count, [None] * count, []
    beside = lax.ppermute(inputs, "col", BESIDE)
    for k in range(count + 1):
        started = []

        def exchange():
            parts = [arrays["across", k - 1]] if k else []
            if k < count:
                parts.append(arrays["own", k])
            both = jnp.concatenate(parts) if len(parts) > 1 else parts[0]
            arrays["up", k], arrays["down", k] = send(both, UP), send(both, DOWN)
            started.extend([("up", k), ("down", k)])

        if k == 0:
            exchange()
            arrays["across", k] = send(arrays["own", k], CROSS)
            pair = jnp.concatenate([inputs, beside])
            copies = jnp.broadcast_to(pair, (4, *pair.shape))
            arrays["up", k], arrays["down", k], copies, arrays["own", 1] = fence(
                arrays["up", k], arrays["down", k], copies, arrays["own", 1]
            )
            mine = lax.all_to_all(copies, "col", 0, 0, axis_index_groups=Y_GROUPS, tiled=True)
            mine = mine.reshape(-1, mine.shape[-1])
            continue
        size = sizes[k - 1]
        first = 2 * sizes[k - 2] if k > 1 else 0
        ready = [
            send(arrays["up", k - 1][first : first + size], UP),
            send(arrays["down", k - 1][first + size : first + 2 * size], DOWN),
        ]
        if k == count:
            exchange()
        made = []
        if k > 1:
            made = multiply((k - 2, FAR))
        last = min(k, count - 1)
        if k < count:
            ready, arrays["across", k - 1], arrays["own", last] = fence(
                ready, arrays["across", k - 1], arrays["own", last]
            )
        if made:
            far[k - 2] = made[0]
            made = [chip_sums(place, near[k - 2], far[k - 2])]
        arrays["far_up", k - 1], arrays["far_down", k - 1] = ready
        if k < count:
            arrays["across_far", k - 1] = send(jnp.concatenate(ready), CROSS)
            started.append(("across_far", k - 1))
        else:
            arrays["last_up", k - 1] = send(arrays["up", k][:size], UP)
            arrays["last_down", k - 1] = send(arrays["down", k][size:], DOWN)
        if k == 1:
            near[0] = multiply((0, NEAR))[0]
        if k < count:
            exchange()
            own_k, near[0] = fence(arrays["own", k], near[0])
            arrays["across", k] = send(own_k, CROSS)
            started.append(("across", k))
        if k == count:
            started = []
        held = [arrays[name] for name in started]
        later = [arrays["own", k + 1]] if k + 1 < count else []
        extra = [mine] if k == 1 else []
        held, later, near, extra, made = fence(held, later, near, extra, made)
        if k == count:
            near[k - 1] = multiply((k - 1, NEAR))[0]
        sums += [sum_direct(chip) for chip in made]
        arrays.update(zip(started, held))
        if later:
            arrays["own", k + 1] = later[0]
        if extra:
            mine = extra[0]
            other = lax.ppermute(mine, "col", CORE)
    far[count - 1] = multiply((count - 1, FAR))[0]
    chip = chip_sums(place, near[-1], far[-1])
    chip, mine, other = fence(chip, mine, other)
    sums.append(sum_direct(chip))
    weight_grad = contract_tokens(place, gathered, groups, mine, other)
    input_grad = jnp.concatenate(sums, axis=0)
    return input_grad, weight_grad


def solution(mesh):
    placed = (P("col", "row"), P("row", "col"), P("row", "col"))
    return jax.shard_map(
        local,
        mesh=mesh,
        in_specs=placed,
        out_specs=(P("col", "row"), P("row", "col")),
        check_vma=False,
    )
```
